32 devices in a mesh: row: 8 (over z, y), col: 4 (over x, core).
Axes of the slice: x: 2, y: 2, z: 4, core: 2. Of those that a mesh axis runs over, the one named last changes fastest.
Arguments:
- amplitudes: float32 [4096, 2048], P('row', 'col'), may hold values from -6 to 6
- integrals: float32 [512, 2048], P('row', 'col'), may hold values from -0.1875 to 0.1875
- owner_order: int32 [512], replicated, may hold values from 0 to 511, each once
Outputs:
- cycle: float32 [512, 4096], P('col', 'row')
The draws below stay inside these ranges and needn't reach their ends.
Inputs may be any that keep to these rules, and one draw needn't show every extreme that they name: owner_order holds each of the 512 result pairs exactly once.
All inputs are finite; a program needn't handle non-finite values.
Results may differ from the reference program's by a relative error of at most 0.00007.
Values sent between devices are 32-bit elements; how exact they have to be, the bound alone decides.
No kernel may reach another device: no remote copies, remote signals or barrier semaphores. Data moves between devices by JAX's collectives and lax.ppermute only.
A program may use at most 64 MiB of HBM per device.

```python
import jax
import jax.numpy as jnp
from jax import lax

I_ALL = 4096
K_ALL = 2048
J_ALL = 512


def strengthened(entries, stream_key, source, target, shards_of, factor):
    owner, partner = [(jnp.arange(entries.shape[position]) // (entries.shape[position] // shards_of)).reshape([-1 if axis == position else 1 for axis in range(entries.ndim)]) for position in (source, target)]
    chosen = jax.random.permutation(stream_key, shards_of)[partner]
    strong = (owner == chosen) | (owner == (partner + shards_of // 2) % shards_of)
    return jnp.where(strong, factor * entries, entries)


def steps_of(key, extent, pieces, least, largest):
    def one(dim, blocks):
        heights = jax.random.uniform(jax.random.fold_in(jax.random.fold_in(key, 6), dim), (blocks,), jnp.float32, least / len(pieces), largest / len(pieces))
        return jnp.repeat(jnp.exp(heights), extent[dim] // blocks).reshape((-1,) + (1,) * (len(extent) - dim - 1))

    loudness = one(*pieces[0])
    for cut in pieces[1:]:
        loudness = loudness * one(*cut)
    return loudness


def centred(key, dims, spread, bound, split=(), held_as=jnp.bfloat16):
    values = spread * jax.random.normal(key, dims, jnp.float32)
    if split:
        values = values * steps_of(key, dims, split, -0.22, 0.18)
    return jnp.clip(values, -bound, bound).astype(held_as)


def bell_draw_with(stream_key, shape, scale, limit, pieces, heavy, kind=jnp.bfloat16):
    entries = scale * jax.random.normal(stream_key, shape, jnp.float32)
    if pieces:
        entries = entries * steps_of(stream_key, shape, pieces, -0.22, 0.18)
    return jnp.clip(strengthened(entries, jax.random.fold_in(stream_key, 3), *heavy), -limit, limit).astype(kind)


def setup_inputs(seed: int = 0) -> dict:
    keys = jax.random.split(jax.random.key(seed), 4)
    return {
        "amplitudes": centred(keys[0], (I_ALL, K_ALL), 1.0, 6.0, ((0, 8), (1, 4)), jnp.float32),
        "integrals": bell_draw_with(keys[1], (J_ALL, K_ALL), K_ALL ** -0.5, 0.1875, ((0, 8), (1, 4)), (1, 0, 8, 2.0), jnp.float32),
        "owner_order": jax.random.permutation(keys[2], J_ALL).astype(jnp.int32),
    }


def reference(amplitudes, integrals, owner_order):
    ordered = jnp.take(integrals, owner_order.astype(jnp.int32), axis=0)
    return lax.dot_general(ordered, amplitudes, (((1,), (1,)), ((), ())), precision=lax.Precision.HIGHEST, preferred_element_type=jnp.float32)
```

```python
import jax
import jax.numpy as jnp
from jax import lax
from jax.experimental import pallas as pl
from jax.experimental.pallas import tpu as pltpu
from jax.sharding import PartitionSpec as P


def halves(x):
    high = x.astype(jnp.bfloat16)
    low = (x - high.astype(jnp.float32)).astype(jnp.bfloat16)
    return high, low


def times(left, right, dims):
    return lax.dot_general(left, right, (dims, ((), ())), preferred_element_type=jnp.float32)


def split_kernel(x_ref, high_ref, low_ref):
    high, low = halves(x_ref[...])
    high_ref[...] = high
    low_ref[...] = low


def split(x):
    shape = jax.ShapeDtypeStruct(x.shape, jnp.bfloat16)
    return pl.pallas_call(
        split_kernel,
        out_shape=(shape, shape),
        cost_estimate=pl.CostEstimate(flops=0, bytes_accessed=2 * x.nbytes, transcendentals=0),
    )(x)


def product_kernel(*refs):
    place_ref, high_ref, low_ref, *blocks, far_ref, near_ref, sel_high, sel_low = refs
    rows = blocks[0].shape[0]
    for m, block in enumerate(blocks):
        high, low = halves(block[...])
        sel_high[m * rows : (m + 1) * rows, :] = high
        sel_low[m * rows : (m + 1) * rows, :] = low
    for h, out in enumerate((far_ref, near_ref)):
        n = out.shape[0]
        place = place_ref[h * n : (h + 1) * n, :]
        column = lax.broadcasted_iota(jnp.int32, (n, rows * len(blocks)), 1)
        pick = jnp.where(column == place, 1.0, 0.0).astype(jnp.bfloat16)
        left_high = times(pick, sel_high[...], ((1,), (0,))).astype(jnp.bfloat16)
        left_low = times(pick, sel_low[...], ((1,), (0,))).astype(jnp.bfloat16)
        total = times(left_high, low_ref[...], ((1,), (1,)))
        total += times(left_low, high_ref[...], ((1,), (1,)))
        total += times(left_high, high_ref[...], ((1,), (1,)))
        out[...] = total


def product(place, high, low, blocks):
    n, width = place.shape[0] // 2, high.shape[0]
    depth = high.shape[1]
    stacked = len(blocks) * blocks[0].shape[0]
    shape = jax.ShapeDtypeStruct((n, width), jnp.float32)
    return pl.pallas_call(
        product_kernel,
        out_shape=(shape, shape),
        scratch_shapes=[pltpu.VMEM((stacked, depth), jnp.bfloat16)] * 2,
        compiler_params=pltpu.CompilerParams(vmem_limit_bytes=32 * 1024 * 1024),
        cost_estimate=pl.CostEstimate(
            flops=2 * n * 2 * depth * (3 * width + 2 * stacked), bytes_accessed=4 * n * width * 2, transcendentals=0
        ),
    )(place, high, low, *blocks)


def solution(mesh):
    rows, cols = mesh.shape["row"], mesh.shape["col"]

    def along(axis, size, m, x):
        return lax.ppermute(x, axis, [(i, i ^ m) for i in range(size)])

    def on_device(amplitudes, integrals, owner_order):
        high, low = split(amplitudes)
        blocks = {0: integrals}
        for m in range(rows - 2, 0, -2):
            blocks[m] = along("row", rows, m, integrals)
        for m in range(0, rows, 2):
            blocks[m + 1] = along("row", rows, 1, blocks[m])
        order = [blocks[m] for m in range(rows)]

        height = integrals.shape[0]
        me, mine = lax.axis_index("row"), lax.axis_index("col")
        local = ((owner_order // height) ^ me) * height + owner_order % height
        share = owner_order.shape[0] // cols
        local = local.reshape(cols, share)
        place = [jnp.take(local, mine ^ m, axis=0, mode="clip").reshape(share, 1) for m in range(cols)]

        out = None
        for m in range(cols - 2, -1, -2):
            other, own = product(jnp.concatenate([place[m + 1], place[m]]), high, low, order)
            own = own + along("col", cols, 1, other)
            if m:
                own = along("col", cols, m, own)
            out = own if out is None else out + own
        return out

    in_specs = (P("row", "col"), P("row", "col"), P())
    out_specs = P("col", "row")
    return jax.shard_map(
        on_device, mesh=mesh, in_specs=in_specs, out_specs=out_specs, check_vma=False
    )
```

```python
import functools

import jax
import jax.numpy as jnp
from jax import lax
from jax.experimental import pallas as pl
from jax.experimental.pallas import tpu as pltpu
from jax.sharding import PartitionSpec as P

MIB = 1024 * 1024


def halves(x):
    high = x.astype(jnp.bfloat16)
    low = (x - high.astype(jnp.float32)).astype(jnp.bfloat16)
    return high, low


def times(left, right):
    return lax.dot_general(left, right, (((1,), (0,)), ((), ())), preferred_element_type=jnp.float32)


def prepare_kernel(x_ref, place_ref, right_ref, pick_ref):
    high, low = halves(x_ref[...].T)
    depth = high.shape[0]
    right_ref[:depth, :] = high
    right_ref[depth : 2 * depth, :] = high
    right_ref[2 * depth :, :] = low
    column = lax.broadcasted_iota(jnp.int32, pick_ref.shape, 1)
    pick_ref[...] = jnp.where(column == place_ref[...], 1.0, 0.0).astype(jnp.bfloat16)


def prepare(amplitudes, place, stacked):
    width, depth = amplitudes.shape
    return pl.pallas_call(
        prepare_kernel,
        out_shape=(
            jax.ShapeDtypeStruct((3 * depth, width), jnp.bfloat16),
            jax.ShapeDtypeStruct((place.shape[0], stacked), jnp.bfloat16),
        ),
        compiler_params=pltpu.CompilerParams(vmem_limit_bytes=8 * MIB),
        cost_estimate=pl.CostEstimate(flops=0, bytes_accessed=4 * MIB, transcendentals=0),
    )(amplitudes, place)


def product_kernel(spots, pick_ref, right_ref, *refs):
    *pieces, other_ref, own_ref, parts, left = refs
    depth = pieces[0].shape[1]
    for piece, moves in zip(pieces, spots):
        for source, target, n in moves:
            high, low = halves(piece[source : source + n, :])
            parts[target : target + n, :depth] = high
            parts[target : target + n, depth:] = low
    chosen = times(pick_ref[...], parts[...]).astype(jnp.bfloat16)
    left[:, : 2 * depth] = chosen
    left[:, 2 * depth :] = chosen[:, :depth]
    total = times(left[...], right_ref[...])
    n = other_ref.shape[0]
    other_ref[...] = total[:n]
    own_ref[...] = total[n:]


def product(pick, right, placed):
    n, stacked = pick.shape
    pieces = [piece for piece, _ in placed]
    spots = [moves for _, moves in placed]
    width, depth = right.shape[1], pieces[0].shape[1]
    shape = jax.ShapeDtypeStruct((n // 2, width), jnp.float32)
    return pl.pallas_call(
        functools.partial(product_kernel, spots),
        out_shape=(shape, shape),
        scratch_shapes=[
            pltpu.VMEM((stacked, 2 * depth), jnp.bfloat16),
            pltpu.VMEM((n, 3 * depth), jnp.bfloat16),
        ],
        compiler_params=pltpu.CompilerParams(vmem_limit_bytes=8 * MIB),
        cost_estimate=pl.CostEstimate(
            flops=2 * n * depth * (3 * width + 2 * stacked), bytes_accessed=4 * MIB, transcendentals=0
        ),
    )(pick, right, *pieces)


def solution(mesh):
    rows, cols = mesh.shape["row"], mesh.shape["col"]

    def along(axis, size, m, x):
        return lax.ppermute(x, axis, [(i, i ^ m) for i in range(size)])

    def on_device(amplitudes, integrals, owner_order):
        height = integrals.shape[0]
        stacked = rows * height
        me, mine = lax.axis_index("row"), lax.axis_index("col")
        local = ((owner_order // height) ^ me) * height + owner_order % height
        share = stacked // cols
        local = local.reshape(cols, share)
        place = jnp.concatenate([jnp.take(local, mine ^ m, axis=0, mode="clip") for m in range(cols - 1, -1, -1)])
        right, pick = prepare(amplitudes, place.reshape(stacked, 1), stacked)

        far = rows // 2
        cut = height // 32 * 16 or height
        near, wide = range(2, far, 2), range(far + 2, rows, 2)
        got = {0: integrals}
        for m in near:
            got[m] = along("row", rows, m, integrals)
        top = along("row", rows, far, integrals[:cut])
        for m in near:
            got[m + 1] = along("row", rows, 1, got[m])
        got[1] = along("row", rows, 1, integrals)
        for m in wide:
            got[m] = along("row", rows, m, integrals)
        if cut < height:
            below = along("row", rows, far, jnp.concatenate([integrals[cut:], got[1][cut:]]))
        for m in wide:
            got[m + 1] = along("row", rows, 1, got[m])
        if near:
            top, got[near[-1] + 1] = lax.optimization_barrier((top, got[near[-1] + 1]))
        top_next = along("row", rows, 1, top)
        order = [0, *near, *[m + 1 for m in wide], *[m + 1 for m in near], *wide]
        placed = [(got[m], [(0, m * height, height)]) for m in order]
        placed.append((top_next, [(0, (far + 1) * height, cut)]))
        placed.append((top, [(0, far * height, cut)]))
        placed.append((got[1], [(0, height, height)]))
        if cut < height:
            rest = height - cut
            placed.append((below, [(0, far * height + cut, rest), (rest, (far + 1) * height + cut, rest)]))

        if height % 16:
            placed.sort(key=lambda item: item[1][0][1])
            placed = [(jnp.concatenate([piece for piece, _ in placed]), [(0, 0, stacked)])]
        sums = []
        for step in range(cols // 2):
            chosen = pick[2 * step * share : 2 * (step + 1) * share]
            other, own = product(chosen, right, placed)
            sums.append(own + along("col", cols, 1, other))
        out = sums.pop()
        for step, total in enumerate(sums):
            out = out + along("col", cols, cols - 2 - 2 * step, total)
        return out

    in_specs = (P("row", "col"), P("row", "col"), P())
    out_specs = P("col", "row")
    return jax.shard_map(
        on_device, mesh=mesh, in_specs=in_specs, out_specs=out_specs, check_vma=False
    )
```

```python
import functools

import jax
import jax.numpy as jnp
from jax import lax
from jax.experimental import pallas as pl
from jax.experimental.pallas import tpu as pltpu
from jax.sharding import PartitionSpec as P

MIB = 1024 * 1024
PARAMS = pltpu.CompilerParams(vmem_limit_bytes=8 * MIB)


def halves(x):
    high = x.astype(jnp.bfloat16)
    low = (x - high.astype(jnp.float32)).astype(jnp.bfloat16)
    return high, low


def times(left, right):
    return lax.dot_general(left, right, (((1,), (0,)), ((), ())), preferred_element_type=jnp.float32)


def cost(flops):
    return pl.CostEstimate(flops=flops, bytes_accessed=4 * MIB, transcendentals=0)


def prepare_kernel(x_ref, place_ref, right_ref, early_ref, late_ref):
    high, low = halves(x_ref[...].T)
    depth = high.shape[0]
    right_ref[:depth, :] = high
    right_ref[depth : 2 * depth, :] = high
    right_ref[2 * depth :, :] = low
    start = 0
    for ref in (early_ref, late_ref):
        column = lax.broadcasted_iota(jnp.int32, ref.shape, 1) + start
        ref[...] = jnp.where(column == place_ref[...], 1.0, 0.0).astype(jnp.bfloat16)
        start += ref.shape[1]


def prepare(amplitudes, place, early, late):
    width, depth = amplitudes.shape
    shapes = ((3 * depth, width), (place.shape[0], early), (place.shape[0], late))
    return pl.pallas_call(
        prepare_kernel,
        out_shape=[jax.ShapeDtypeStruct(shape, jnp.bfloat16) for shape in shapes],
        compiler_params=PARAMS,
        cost_estimate=cost(0),
    )(amplitudes, place)


def stack(pieces, parts):
    depth, start = pieces[0].shape[1], 0
    for piece in pieces:
        high, low = halves(piece[...])
        stop = start + piece.shape[0]
        parts[start:stop, :depth] = high
        parts[start:stop, depth:] = low
        start = stop


def choose_kernel(pick_ref, *refs):
    *pieces, out_ref, parts = refs
    stack(pieces, parts)
    out_ref[...] = times(pick_ref[...], parts[...]).astype(jnp.bfloat16)


def choose(pick, pieces):
    n, stacked = pick.shape
    depth = pieces[0].shape[1]
    return pl.pallas_call(
        choose_kernel,
        out_shape=jax.ShapeDtypeStruct((n, 2 * depth), jnp.bfloat16),
        scratch_shapes=[pltpu.VMEM((stacked, 2 * depth), jnp.bfloat16)],
        compiler_params=PARAMS,
        cost_estimate=cost(4 * n * stacked * depth),
    )(pick, *pieces)


def product_kernel(start, pieces_count, chosen_ref, pick_ref, right_ref, *refs):
    pieces = refs[:pieces_count]
    *outs, parts, left = refs[pieces_count:]
    stack(pieces, parts)
    n = left.shape[0]
    chosen = times(pick_ref[start : start + n, :], parts[...]) + chosen_ref[start : start + n, :].astype(jnp.float32)
    chosen = chosen.astype(jnp.bfloat16)
    depth = left.shape[1] // 3
    left[:, : 2 * depth] = chosen
    left[:, 2 * depth :] = chosen[:, :depth]
    total = times(left[...], right_ref[...])
    share = n // len(outs)
    for i, out in enumerate(outs):
        out[...] = total[i * share : (i + 1) * share]


def product(chosen, pick, right, pieces, start, share, count):
    depth, width = pieces[0].shape[1], right.shape[1]
    n = share * count
    return pl.pallas_call(
        functools.partial(product_kernel, start, len(pieces)),
        out_shape=[jax.ShapeDtypeStruct((share, width), jnp.float32)] * count,
        scratch_shapes=[
            pltpu.VMEM((pick.shape[1], 2 * depth), jnp.bfloat16),
            pltpu.VMEM((n, 3 * depth), jnp.bfloat16),
        ],
        compiler_params=PARAMS,
        cost_estimate=cost(2 * n * depth * (3 * width + 2 * pick.shape[1])),
    )(chosen, pick, right, *pieces)


def solution(mesh):
    rows, cols = mesh.shape["row"], mesh.shape["col"]

    def along(axis, size, m, x):
        return lax.ppermute(x, axis, [(i, i ^ m) for i in range(size)])

    def on_device(amplitudes, integrals, owner_order):
        height = integrals.shape[0]
        stacked = rows * height
        me, mine = lax.axis_index("row"), lax.axis_index("col")

        far = rows // 2
        cut = height // 32 * 16 or height
        rest = height - cut
        near, wide = range(2, far, 2), range(far + 2, rows, 2)

        straight = [*near, 0, *wide, 1]
        forwarded = [m + 1 for m in (*near, *wide)]
        upper, lower = [0] * rows, [0] * rows
        at = 0
        for m in straight:
            upper[m], lower[m] = at, at + cut
            at += height
        upper[far] = at
        early = at = at + cut
        lower[far], lower[far + 1] = at, at + rest
        at += 2 * rest
        for m in forwarded:
            upper[m], lower[m] = at, at + cut
            at += height
        upper[far + 1] = at

        block, row = (owner_order // height) ^ me, owner_order % height
        place = row
        for m in range(rows):
            place = place + jnp.where(block == m, jnp.where(row < cut, upper[m], lower[m] - cut), 0)
        share = stacked // cols
        place = place.reshape(cols, share)
        place = jnp.concatenate([jnp.take(place, mine ^ m, axis=0, mode="clip") for m in range(cols - 1, -1, -1)])
        prepared = prepare(amplitudes, place.reshape(stacked, 1), early, stacked - early)

        got = {0: integrals}
        got[1] = along("row", rows, 1, integrals)
        for m in wide:
            got[m] = along("row", rows, m, integrals)
        top = along("row", rows, far, integrals[:cut])
        for m in near:
            got[m] = along("row", rows, m, integrals)
        for m in near:
            got[m + 1] = along("row", rows, 1, got[m])
        to_forward, right, pick_early, pick_late = lax.optimization_barrier((top, *prepared))
        top_next = along("row", rows, 1, to_forward)
        below = []
        if rest:
            below.append(along("row", rows, far, jnp.concatenate([integrals[cut:], got[1][cut:]])))
        for m in wide:
            got[m + 1] = along("row", rows, 1, got[m])
        first = [*[got[m] for m in straight], top]
        last = [*below, *[got[m] for m in forwarded], top_next]
        if height % 16:
            first, last = [jnp.concatenate(first)], [jnp.concatenate(last)]
        chosen = choose(pick_early, first)

        def sums(start, count):
            return product(chosen, pick_late, right, last, start * share, share, count)

        moved = []
        for t in range(0, cols - 2, 2):
            (other,) = sums(t, 1)
            own, *home = sums(t + 1, 3 if t == cols - 4 else 1)
            moved.append(along("col", cols, cols - 2 - t, own + along("col", cols, 1, other)))
        other, own = home if moved else sums(0, 2)
        out = own + along("col", cols, 1, other)
        for x in moved:
            out = out + x
        return out

    in_specs = (P("row", "col"), P("row", "col"), P())
    out_specs = P("col", "row")
    return jax.shard_map(
        on_device, mesh=mesh, in_specs=in_specs, out_specs=out_specs, check_vma=False
    )
```

```python
import functools

import jax
import jax.numpy as jnp
from jax import lax
from jax.experimental import pallas as pl
from jax.experimental.pallas import tpu as pltpu
from jax.sharding import PartitionSpec as P

MIB = 1024 * 1024
PARAMS = pltpu.CompilerParams(vmem_limit_bytes=8 * MIB)


def halves(x):
    high = x.astype(jnp.bfloat16)
    low = (x - high.astype(jnp.float32)).astype(jnp.bfloat16)
    return high, low


def times(left, right):
    return lax.dot_general(left, right, (((1,), (0,)), ((), ())), preferred_element_type=jnp.float32)


def cost(flops):
    return pl.CostEstimate(flops=flops, bytes_accessed=4 * MIB, transcendentals=0)


def lay_out_kernel(x_ref, right_ref):
    high, low = halves(x_ref[...].T)
    depth = high.shape[0]
    right_ref[:depth, :] = high
    right_ref[depth : 2 * depth, :] = high
    right_ref[2 * depth :, :] = low


def lay_out(amplitudes):
    width, depth = amplitudes.shape
    return pl.pallas_call(
        lay_out_kernel,
        out_shape=jax.ShapeDtypeStruct((3 * depth, width), jnp.bfloat16),
        compiler_params=PARAMS,
        cost_estimate=cost(0),
    )(amplitudes)


def name_kernel(place_ref, early_ref, late_ref):
    start = 0
    for ref in (early_ref, late_ref):
        column = lax.broadcasted_iota(jnp.int32, ref.shape, 1) + start
        ref[...] = jnp.where(column == place_ref[...], 1.0, 0.0).astype(jnp.bfloat16)
        start += ref.shape[1]


def name_rows(place, early, late):
    n = place.shape[0]
    return pl.pallas_call(
        name_kernel,
        out_shape=[jax.ShapeDtypeStruct((n, width), jnp.bfloat16) for width in (early, late)],
        compiler_params=PARAMS,
        cost_estimate=cost(0),
    )(place)


def stack(pieces, parts):
    depth, start = pieces[0].shape[1], 0
    for piece in pieces:
        high, low = halves(piece[...])
        stop = start + piece.shape[0]
        parts[start:stop, :depth] = high
        parts[start:stop, depth:] = low
        start = stop


def choose_kernel(pick_ref, *refs):
    *pieces, out_ref, parts = refs
    stack(pieces, parts)
    out_ref[...] = times(pick_ref[...], parts[...]).astype(jnp.bfloat16)


def choose(pick, pieces):
    n, stacked = pick.shape
    depth = pieces[0].shape[1]
    return pl.pallas_call(
        choose_kernel,
        out_shape=jax.ShapeDtypeStruct((n, 2 * depth), jnp.bfloat16),
        scratch_shapes=[pltpu.VMEM((stacked, 2 * depth), jnp.bfloat16)],
        compiler_params=PARAMS,
        cost_estimate=cost(4 * n * stacked * depth),
    )(pick, *pieces)


def product_kernel(start, pieces_count, chosen_ref, pick_ref, right_ref, *refs):
    pieces = refs[:pieces_count]
    *outs, parts, left = refs[pieces_count:]
    stack(pieces, parts)
    n = left.shape[0]
    chosen = times(pick_ref[start : start + n, :], parts[...]) + chosen_ref[start : start + n, :].astype(jnp.float32)
    chosen = chosen.astype(jnp.bfloat16)
    depth = left.shape[1] // 3
    left[:, : 2 * depth] = chosen
    left[:, 2 * depth :] = chosen[:, :depth]
    total = times(left[...], right_ref[...])
    share = n // len(outs)
    for i, out in enumerate(outs):
        out[...] = total[i * share : (i + 1) * share]


def product(chosen, pick, right, pieces, start, share, count):
    depth, width = pieces[0].shape[1], right.shape[1]
    n = share * count
    return pl.pallas_call(
        functools.partial(product_kernel, start, len(pieces)),
        out_shape=[jax.ShapeDtypeStruct((share, width), jnp.float32)] * count,
        scratch_shapes=[
            pltpu.VMEM((pick.shape[1], 2 * depth), jnp.bfloat16),
            pltpu.VMEM((n, 3 * depth), jnp.bfloat16),
        ],
        compiler_params=PARAMS,
        cost_estimate=cost(2 * n * depth * (3 * width + 2 * pick.shape[1])),
    )(chosen, pick, right, *pieces)


def solution(mesh):
    rows, cols = mesh.shape["row"], mesh.shape["col"]

    def along(axis, size, m, x):
        return lax.ppermute(x, axis, [(i, i ^ m) for i in range(size)])

    def on_device(amplitudes, integrals, owner_order):
        height = integrals.shape[0]
        stacked = rows * height
        me, mine = lax.axis_index("row"), lax.axis_index("col")

        far = rows // 2
        cut = height // 32 * 16 or height
        rest = height - cut
        near, wide = range(2, far, 2), range(far + 2, rows, 2)

        straight = [*near, 0, *wide, 1]
        forwarded = [m + 1 for m in (*near, *wide)]
        upper, lower = [0] * rows, [0] * rows
        at = 0
        for m in straight:
            upper[m], lower[m] = at, at + cut
            at += height
        upper[far] = at
        early = at = at + cut
        lower[far], lower[far + 1] = at, at + rest
        at += 2 * rest
        for m in forwarded:
            upper[m], lower[m] = at, at + cut
            at += height
        upper[far + 1] = at

        block, row = (owner_order // height) ^ me, owner_order % height
        place = row
        for m in range(rows):
            place = place + jnp.where(block == m, jnp.where(row < cut, upper[m], lower[m] - cut), 0)
        share = stacked // cols
        place = place.reshape(cols, share)
        place = jnp.concatenate([jnp.take(place, mine ^ m, axis=0, mode="clip") for m in range(cols - 1, -1, -1)])
        right = lay_out(amplitudes)
        picks = name_rows(place.reshape(stacked, 1), early, stacked - early)

        got = {0: integrals}
        got[1] = along("row", rows, 1, integrals)
        for m in wide:
            got[m] = along("row", rows, m, integrals)
        top = along("row", rows, far, integrals[:cut])
        for m in near:
            got[m] = along("row", rows, m, integrals)
        for m in near:
            got[m + 1] = along("row", rows, 1, got[m])
        to_forward, pick_early, pick_late = lax.optimization_barrier((top, *picks))
        top_next = along("row", rows, 1, to_forward)
        below = []
        if rest:
            below.append(along("row", rows, far, jnp.concatenate([integrals[cut:], got[1][cut:]])))
        for m in wide:
            got[m + 1] = along("row", rows, 1, got[m])
        first = [*[got[m] for m in straight], top]
        last = [*below, *[got[m] for m in forwarded], top_next]
        if height % 16:
            first, last = [jnp.concatenate(first)], [jnp.concatenate(last)]
        chosen = choose(pick_early, first)

        def sums(start, count):
            return product(chosen, pick_late, right, last, start * share, share, count)

        moved = []
        for t in range(0, cols - 2, 2):
            (other,) = sums(t, 1)
            own, *home = sums(t + 1, 3 if t == cols - 4 else 1)
            moved.append(along("col", cols, cols - 2 - t, own + along("col", cols, 1, other)))
        other, own = home if moved else sums(0, 2)
        out = own + along("col", cols, 1, other)
        for x in moved:
            out = out + x
        return out

    in_specs = (P("row", "col"), P("row", "col"), P())
    out_specs = P("col", "row")
    return jax.shard_map(
        on_device, mesh=mesh, in_specs=in_specs, out_specs=out_specs, check_vma=False
    )
```
